32 devices in a mesh: dm: 4 (over y, core), df: 8 (over z, x).
Axes of the slice: x: 2, y: 2, z: 4, core: 2. Of those that a mesh axis runs over, the one named last changes fastest.
Arguments:
- hidden_in: bfloat16 [16, 14848], P(None, 'dm'), may hold values from -30 to 30
- attn_gain: float32 [14848], P('dm'), may hold values from 0.1 to 1.9
- attn_bias: float32 [14848], P('dm'), may hold values from -3 to 3
- mlp_gain: float32 [14848], P('dm'), may hold values from 0.1 to 1.9
- mlp_bias: float32 [14848], P('dm'), may hold values from -3 to 3
- w_query: bfloat16 [14848, 8192], P('dm', 'df'), may hold values from -0.046875 to 0.046875
- query_exp: int32 [464, 8192], P('dm', 'df'), may hold values from -2 to 1
- w_keyval: bfloat16 [14848, 1024], P('dm', 'df'), may hold values from -0.046875 to 0.046875
- keyval_exp: int32 [464, 1024], P('dm', 'df'), may hold values from -2 to 1
- w_out: bfloat16 [8192, 14848], P('df', 'dm'), may hold values from -0.09375 to 0.09375
- out_exp: int32 [256, 14848], P('df', 'dm'), may hold values from -2 to 1
- w_up: bfloat16 [14848, 29696], P('dm', 'df'), may hold values from -0.046875 to 0.046875
- up_exp: int32 [464, 29696], P('dm', 'df'), may hold values from -2 to 1
- w_down: bfloat16 [29696, 14848], P('df', 'dm'), may hold values from -0.046875 to 0.046875
- down_exp: int32 [928, 14848], P('df', 'dm'), may hold values from -2 to 1
- kv_cache: bfloat16 [16, 65536, 128], P('dm', 'df'), may hold values from -384 to 384
- lengths: int32 [16], P('dm'), may hold values from 2 to 8192, as said below
- positions: int32 [16], P('dm'), may hold values from 0 to 32767
Outputs:
- mixed: bfloat16 [16, 14848], P(None, ('dm', 'df'))
The draws below stay inside these ranges and needn't reach their ends.
Inputs may be any that keep to these rules, and one draw needn't show every extreme that they name: `lengths`: some row uses all 8192 slots.
All inputs are finite; a program needn't handle non-finite values.
Results may differ from the reference program's by a relative error of at most 0.013.
The reference program's roundings to bfloat16 on the way count: a program that leaves them out, or rounds other values in their place, can miss the bound.
Values may be sent and summed in bfloat16 or wider, within the bound.
A program may use at most 256 MiB of HBM per device.

```python
import math
import jax
import jax.numpy as jnp
from jax import lax

D = 14848
FF = 29696
HEADS = 128
KV = 8
HD = 64
CTX = 8192
ROWS = 16


def row_lengths(key):
    inner = jax.random.fold_in(key, 13)
    first, second = jax.random.split(inner, 2)
    values = jax.random.randint(first, (ROWS,), 2, CTX + 1, jnp.int32)
    chosen = jax.random.randint(second, (), 0, ROWS, jnp.int32)
    return jnp.where(jnp.arange(ROWS, dtype=jnp.int32) == chosen, CTX, values).astype(jnp.int32)


def draw_hidden_in(key, part):
    key = jax.random.fold_in(key, 11)
    first, second = jax.random.split(key, 2)
    ramp = 0.5 * 3.0 ** (jnp.arange(D, dtype=jnp.float32) / D)
    base = jax.random.truncated_normal(first, -4.0, 4.0, (ROWS, D), jnp.float32)
    row_scale = jnp.exp(jax.random.uniform(second, (ROWS, 1), jnp.float32, jnp.log(0.5), jnp.log(2.0)))
    return (base * ramp[None, :] * row_scale).astype(jnp.bfloat16)


def draw_kv_cache(key, part):
    key = jax.random.fold_in(key, 12)
    first = jax.random.fold_in(key, 0)
    base = jax.random.truncated_normal(first, -4.0, 4.0, (ROWS, KV * CTX, 2 * HD), jnp.float32)
    return base.astype(jnp.bfloat16)


def draw_lengths(key, part):
    return row_lengths(key)


def set_ends(values, stream_key, low, top_value):
    shape = values.shape
    index_at = [jax.random.randint(jax.random.fold_in(stream_key, axis), (), 0, shape[axis]) for axis in range(len(shape))]
    values = values.at[tuple(index_at)].set(low)
    longest = shape.index(max(shape))
    index_at[longest] = (index_at[longest] + 1) % shape[longest]
    return values.at[tuple(index_at)].set(top_value)


def raised(array, stream_key, source, target, shards_of, factor):
    owner, partner = [(jnp.arange(array.shape[axis_at]) // (array.shape[axis_at] // shards_of)).reshape([-1 if axis == axis_at else 1 for axis in range(array.ndim)]) for axis_at in (source, target)]
    chosen = jax.random.permutation(stream_key, shards_of)[partner]
    strong = (owner == chosen) | (owner == (partner + shards_of // 2) % shards_of)
    return jnp.where(strong, factor * array, array)


def block_scale(own_key, dims, shards, low, high):
    def one(axis_at, blocks):
        draws = jax.random.uniform(jax.random.fold_in(jax.random.fold_in(own_key, 6), axis_at), (blocks,), jnp.float32, low / len(shards), high / len(shards))
        return jnp.repeat(jnp.exp(draws), dims[axis_at] // blocks).reshape((-1,) + (1,) * (len(dims) - axis_at - 1))

    loudness = one(*shards[0])
    for cut in shards[1:]:
        loudness = loudness * one(*cut)
    return loudness


def scatter_about(key, shape, width, reach, cuts=(), kind=jnp.bfloat16):
    values = jax.random.normal(key, shape, jnp.float32) * width
    if len(cuts) > 0:
        values = block_scale(key, shape, cuts, -0.22, 0.18) * values
    return jnp.clip(values, min=-reach, max=reach).astype(kind)


def heavy_noise(rng, dims, deviation, reach, pieces, heavy, kind=jnp.bfloat16):
    drawn = deviation * jax.random.normal(rng, dims, jnp.float32)
    if pieces:
        drawn = drawn * block_scale(rng, dims, pieces, -0.22, 0.18)
    return jnp.clip(raised(drawn, jax.random.fold_in(rng, 3), *heavy), -reach, reach).astype(kind)


def setup_inputs(seed: int = 0) -> dict:
    splits = jax.random.split(jax.random.key(seed), 19)
    hidden_in = draw_hidden_in(jax.random.fold_in(splits[18], 71), 0)
    attn_gain = jnp.clip(1.0 + 0.18 * jax.random.normal(splits[1], (D,), jnp.float32), 0.1, 1.9)
    attn_bias = scatter_about(splits[2], (D,), 0.5, 3.0, ((0, 4),), jnp.float32)
    mlp_gain = jnp.clip(1.0 + 0.18 * jax.random.normal(splits[3], (D,), jnp.float32), 0.1, 1.9)
    mlp_bias = scatter_about(splits[4], (D,), 0.5, 3.0, ((0, 4),), jnp.float32)
    w_query = scatter_about(splits[5], (D, HEADS * HD), D ** -0.5, 0.046875, ((0, 4), (1, 8)))
    query_exp = set_ends(jax.random.randint(splits[6], (D // 32, HEADS * HD), -2, 2), jax.random.fold_in(splits[6], 1), -2, 1).astype(jnp.int32)
    w_keyval = scatter_about(splits[7], (D, 2 * KV * HD), D ** -0.5, 0.046875, ((0, 4), (1, 8)))
    keyval_exp = set_ends(jax.random.randint(splits[8], (D // 32, 2 * KV * HD), -2, 2), jax.random.fold_in(splits[8], 1), -2, 1).astype(jnp.int32)
    w_out = heavy_noise(splits[9], (HEADS * HD, D), (HEADS * HD) ** -0.5, 0.09375, ((0, 8), (1, 4)), (0, 1, 8, 2.0))
    out_exp = set_ends(jax.random.randint(splits[10], (HEADS * HD // 32, D), -2, 2), jax.random.fold_in(splits[10], 1), -2, 1).astype(jnp.int32)
    w_up = scatter_about(splits[11], (D, FF), D ** -0.5, 0.046875, ((0, 4), (1, 8)))
    up_exp = set_ends(jax.random.randint(splits[12], (D // 32, FF), -2, 2), jax.random.fold_in(splits[12], 1), -2, 1).astype(jnp.int32)
    w_down = heavy_noise(splits[13], (FF, D), FF ** -0.5, 0.046875, ((0, 8), (1, 4)), (0, 1, 8, 2.0))
    down_exp = set_ends(jax.random.randint(splits[14], (FF // 32, D), -2, 2), jax.random.fold_in(splits[14], 1), -2, 1).astype(jnp.int32)
    kv_cache = draw_kv_cache(jax.random.fold_in(splits[18], 71), 0)
    lengths = draw_lengths(jax.random.fold_in(splits[18], 71), 0)
    positions = set_ends(jax.random.randint(splits[17], (ROWS,), 0, 32768), jax.random.fold_in(splits[17], 1), 0, 32767).astype(jnp.int32)
    return dict(hidden_in=hidden_in, attn_gain=attn_gain, attn_bias=attn_bias, mlp_gain=mlp_gain, mlp_bias=mlp_bias, w_query=w_query, query_exp=query_exp, w_keyval=w_keyval, keyval_exp=keyval_exp, w_out=w_out, out_exp=out_exp, w_up=w_up, up_exp=up_exp, w_down=w_down, down_exp=down_exp, kv_cache=kv_cache, lengths=lengths, positions=positions)


epsilon = 1e-05

def powers(exponents):
    return jnp.where(exponents == -2, 0.25, jnp.where(exponents == -1, 0.5, jnp.where(exponents == 0, 1.0, 2.0))).astype(jnp.bfloat16)

def scaled_product(left, weight, exponents):
    depth, width_out = weight.shape
    row_count = left.shape[0]
    slabs = weight.reshape(depth // 32, 32, width_out)
    left_slabs = left.reshape(row_count, depth // 32, 32).transpose(1, 0, 2)

    def advance(running, item):
        left_part, weight_part, exponent_part = item
        scaled = weight_part * powers(exponent_part)[None, :]
        return (running + jnp.dot(left_part, scaled, preferred_element_type=jnp.float32), None)
    result, unused = lax.scan(advance, jnp.zeros((row_count, width_out), jnp.float32), (left_slabs, slabs, exponents))
    return result

def rotate(values, places):
    half = HD // 2
    freqs = jnp.power(10000.0, -2.0 * jnp.arange(half, dtype=jnp.float32) / HD)
    angles = places.astype(jnp.float32)[:, None] * freqs[None, :]
    cosine = jnp.cos(angles)[:, None, :]
    sine = jnp.sin(angles)[:, None, :]
    first_half = values[..., :half]
    second_half = values[..., half:]
    return jnp.concatenate([first_half * cosine - second_half * sine, second_half * cosine + first_half * sine], axis=-1)

def layer_norm(wide, gain, shift):
    mean_value = lax.optimization_barrier(jnp.mean(wide, axis=1, keepdims=True))
    square_mean = lax.optimization_barrier(jnp.mean(wide * wide, axis=1, keepdims=True))
    inverse = lax.rsqrt(square_mean - mean_value * mean_value + epsilon)
    return ((wide - mean_value) * inverse * gain + shift).astype(jnp.bfloat16)

def reference(hidden_in, attn_gain, attn_bias, mlp_gain, mlp_bias, w_query, query_exp, w_keyval, keyval_exp, w_out, out_exp, w_up, up_exp, w_down, down_exp, kv_cache, lengths, positions):
    wide = hidden_in.astype(jnp.float32)
    attn_in = layer_norm(wide, attn_gain, attn_bias)
    mlp_in = layer_norm(wide, mlp_gain, mlp_bias)
    query_part = scaled_product(attn_in, w_query, query_exp)
    keyval_part = scaled_product(attn_in, w_keyval, keyval_exp).reshape(ROWS, KV, 2, HD)
    queries = rotate(query_part.reshape(ROWS, HEADS, HD), positions).astype(jnp.bfloat16)
    new_keys = rotate(keyval_part[:, :, 0], positions).astype(jnp.bfloat16)
    new_values = keyval_part[:, :, 1].astype(jnp.bfloat16)
    group_size = HEADS // KV
    grouped = queries.reshape(ROWS, group_size, KV, HD).transpose(0, 2, 1, 3).astype(jnp.float32)
    cache = kv_cache.reshape(ROWS, KV, CTX, 2 * HD)
    cache_keys = cache[..., :HD].astype(jnp.float32)
    cache_values = cache[..., HD:].astype(jnp.float32)
    factor = 1.0 / math.sqrt(HD)
    scores = jnp.einsum('rkgd,rkcd->rkgc', grouped, cache_keys) * factor
    live = (jnp.arange(CTX, dtype=jnp.int32)[None, :] < lengths[:, None])[:, None, None, :]
    scores = jnp.where(live, scores, -1e+30)
    own_scores = jnp.einsum('rkgd,rkd->rkg', grouped, new_keys.astype(jnp.float32)) * factor
    top_score = jnp.maximum(lax.optimization_barrier(jnp.max(scores, axis=-1)), own_scores)
    weights = jnp.where(live, jnp.exp(scores - top_score[..., None]), 0.0)
    own_weights = jnp.exp(own_scores - top_score)
    denominator = lax.optimization_barrier(jnp.sum(weights, axis=-1)) + own_weights
    rounded = lax.optimization_barrier(weights.astype(jnp.bfloat16)).astype(jnp.float32)
    own_rounded = lax.optimization_barrier(own_weights.astype(jnp.bfloat16)).astype(jnp.float32)
    summed = jnp.einsum('rkgc,rkcd->rkgd', rounded, cache_values) + own_rounded[..., None] * new_values.astype(jnp.float32)[:, :, None, :]
    attended = (summed / denominator[..., None]).transpose(0, 2, 1, 3).reshape(ROWS, HEADS * HD).astype(jnp.bfloat16)
    attention_out = scaled_product(attended, w_out, out_exp)
    activated = jax.nn.gelu(scaled_product(mlp_in, w_up, up_exp), approximate=False).astype(jnp.bfloat16)
    return (wide + attention_out + scaled_product(activated, w_down, down_exp)).astype(jnp.bfloat16)
```

```python
import functools
import math

import jax
import jax.numpy as jnp
from jax import lax
from jax.experimental import pallas as pl
from jax.experimental.pallas import tpu as pltpu
from jax.sharding import PartitionSpec as P

D = 14848
HEADS = 128
KV = 8
HD = 64


epsilon = 1e-05


def merged(part, axis, combine):
    gathered = jax.tree.map(lambda a: lax.all_gather(a, axis), part)

    def take(source):
        return jax.tree.map(lambda a: lax.dynamic_index_in_dim(a, source, 0, False), gathered)

    return lax.fori_loop(
        1, lax.axis_size(axis), lambda source, state: combine(state, take(source)), take(0)
    )


def powers(exponents):
    return jnp.where(
        exponents == -2, 0.25, jnp.where(exponents == -1, 0.5, jnp.where(exponents == 0, 1.0, 2.0))
    ).astype(jnp.bfloat16)


def dequantize(weight, exponents):
    depth, width_out = weight.shape
    slabs = weight.reshape(depth // 32, 32, width_out) * powers(exponents)[:, None, :]
    return slabs.reshape(depth, width_out)


def rotate(values, places):
    half = HD // 2
    freqs = jnp.power(10000.0, -2.0 * jnp.arange(half, dtype=jnp.float32) / HD)
    angles = places.astype(jnp.float32)[:, None] * freqs[None, :]
    cosine = jnp.cos(angles)[:, None, :]
    sine = jnp.sin(angles)[:, None, :]
    first_half = values[..., :half]
    second_half = values[..., half:]
    return jnp.concatenate(
        [first_half * cosine - second_half * sine, second_half * cosine + first_half * sine],
        axis=-1,
    )


def join_parts(earlier, later):
    top_early, den_early, acc_early = earlier
    top_late, den_late, acc_late = later
    highest = jnp.maximum(top_early, top_late)
    fade_early = jnp.exp(top_early - highest)
    fade_late = jnp.exp(top_late - highest)
    return (
        highest,
        den_early * fade_early + den_late * fade_late,
        acc_early * fade_early[..., None] + acc_late * fade_late[..., None],
    )


def on_device(
    hidden_in,
    attn_gain,
    attn_bias,
    mlp_gain,
    mlp_bias,
    w_query,
    query_exp,
    w_keyval,
    keyval_exp,
    w_out,
    out_exp,
    w_up,
    up_exp,
    w_down,
    down_exp,
    kv_cache,
    lengths,
    positions,
):
    row_count, local_width = hidden_in.shape
    wide = hidden_in.astype(jnp.float32)
    total_sum, square_sum = lax.psum((jnp.sum(wide, axis=1), jnp.sum(wide * wide, axis=1)), "dm")
    mean_value = (total_sum / D)[:, None]
    inverse = lax.rsqrt(square_sum[:, None] / D - mean_value * mean_value + epsilon)
    normed = (wide - mean_value) * inverse
    attn_in = (normed * attn_gain + attn_bias).astype(jnp.bfloat16)
    mlp_in = (normed * mlp_gain + mlp_bias).astype(jnp.bfloat16)
    query_w = dequantize(w_query, query_exp)
    keyval_w = dequantize(w_keyval, keyval_exp)
    query_cols = query_w.shape[1]
    part_rows = row_count // lax.axis_size("dm")
    projected = lax.psum_scatter(
        jnp.concatenate(
            [
                jnp.dot(attn_in, query_w, preferred_element_type=jnp.float32),
                jnp.dot(attn_in, keyval_w, preferred_element_type=jnp.float32),
            ],
            axis=1,
        ),
        "dm",
        scatter_dimension=0,
        tiled=True,
    )
    query_all, keyval_all = (
        lax.all_gather(projected[:, :query_cols], "df", axis=1, tiled=True),
        lax.all_gather(projected[:, query_cols:], "df", axis=1, tiled=True),
    )
    queries = rotate(query_all.reshape(part_rows, HEADS, HD), positions).astype(jnp.bfloat16)
    keyval_new = keyval_all.reshape(part_rows, KV, 2, HD)
    new_keys = rotate(keyval_new[:, :, 0], positions).astype(jnp.bfloat16)
    new_values = keyval_new[:, :, 1].astype(jnp.bfloat16)
    head_devices = lax.axis_size("df")
    blocks = head_devices // KV
    column = lax.axis_index("df")
    group = column // blocks
    block = column % blocks
    group_size = HEADS // KV
    heads_each = HEADS // head_devices
    slots = kv_cache.shape[1]
    factor = 1.0 / math.sqrt(HD)
    query_group = lax.dynamic_slice_in_dim(
        queries.reshape(part_rows, group_size, KV, HD), group, 1, 2
    )[:, :, 0]
    key_one = lax.dynamic_slice_in_dim(new_keys, group, 1, 1)[:, 0]
    value_one = lax.dynamic_slice_in_dim(new_values, group, 1, 1)[:, 0]
    cache_keys = kv_cache[:, :, :HD]
    cache_values = kv_cache[:, :, HD:]
    scores = (
        jnp.einsum("rgd,rcd->rgc", query_group, cache_keys, preferred_element_type=jnp.float32)
        * factor
    )
    places = block * slots + jnp.arange(slots, dtype=jnp.int32)
    live = (places[None, :] < lengths[:, None])[:, None, :]
    scores = jnp.where(live, scores, -1e30)
    leading = block == 0
    own_scores = (
        jnp.einsum("rgd,rd->rg", query_group, key_one, preferred_element_type=jnp.float32) * factor
    )
    own_scores = jnp.where(leading, own_scores, -1e30)
    top_score = jnp.maximum(jnp.max(scores, axis=-1), own_scores)
    weights = jnp.where(live, jnp.exp(scores - top_score[..., None]), 0.0)
    own_weights = jnp.where(leading, jnp.exp(own_scores - top_score), 0.0)
    denominator = jnp.sum(weights, axis=-1) + own_weights
    summed = jnp.einsum(
        "rgc,rcd->rgd",
        weights.astype(jnp.bfloat16),
        cache_values,
        preferred_element_type=jnp.float32,
    )
    summed = (
        summed
        + own_weights.astype(jnp.bfloat16).astype(jnp.float32)[..., None]
        * value_one.astype(jnp.float32)[:, None, :]
    )
    selector = jnp.arange(KV, dtype=jnp.int32) == group
    acc_full = jnp.where(selector[None, None, :, None], summed[:, :, None, :], 0.0).reshape(
        part_rows, HEADS, HD
    )
    top_full = jnp.where(selector[None, None, :], top_score[:, :, None], -1e30).reshape(
        part_rows, HEADS
    )
    den_full = jnp.where(selector[None, None, :], denominator[:, :, None], 0.0).reshape(
        part_rows, HEADS
    )
    top_all, den_all, acc_all = merged((top_full, den_full, acc_full), "df", join_parts)
    own_acc = lax.dynamic_slice_in_dim(acc_all, column * heads_each, heads_each, 1)
    own_den = lax.dynamic_slice_in_dim(den_all, column * heads_each, heads_each, 1)
    attended = (
        (own_acc / own_den[..., None]).reshape(part_rows, heads_each * HD).astype(jnp.bfloat16)
    )
    out_w = dequantize(w_out, out_exp)
    attention_part = jnp.dot(
        lax.all_gather(attended, "dm", axis=0, tiled=True),
        out_w,
        preferred_element_type=jnp.float32,
    )
    up_w = dequantize(w_up, up_exp)
    down_w = dequantize(w_down, down_exp)
    up_total = lax.psum(jnp.dot(mlp_in, up_w, preferred_element_type=jnp.float32), "dm")
    activated = jax.nn.gelu(up_total, approximate=False).astype(jnp.bfloat16)
    feed_part = jnp.dot(activated, down_w, preferred_element_type=jnp.float32)
    layer_total = lax.psum_scatter(
        attention_part + feed_part, "df", scatter_dimension=1, tiled=True
    )
    slice_width = local_width // head_devices
    residual = lax.dynamic_slice_in_dim(wide, column * slice_width, slice_width, 1)
    return (residual + layer_total).astype(jnp.bfloat16)


BLOCK = 32
DEEP = 1024
TILE = 256
LANES = 128
F32 = jnp.float32
BF16 = jnp.bfloat16


def pieces(length, step):
    return [(at, min(step, length - at)) for at in range(0, length, step)]


def powers_wide(exponents):
    return jnp.where(
        exponents == -2, 0.25, jnp.where(exponents == -1, 0.5, jnp.where(exponents == 0, 1.0, 2.0))
    )


def scaled_tile(left, w_ref, e_ref, start, depth, at, width):
    total = None
    for low, span in pieces(depth, TILE):
        exps = e_ref[pl.ds((start + low) // BLOCK, span // BLOCK), pl.ds(at, width)]
        scale = jnp.broadcast_to(
            powers_wide(exps)[:, None, :], (span // BLOCK, BLOCK, width)
        ).astype(BF16).reshape(span, width)
        weight = w_ref[pl.ds(start + low, span), pl.ds(at, width)] * scale
        part = jnp.dot(left[:, low:low + span], weight, preferred_element_type=F32)
        total = part if total is None else total + part
    return total


def scaled_into(acc_ref, offset, first, left, w_ref, e_ref, start, depth, columns):
    def one(at, width):
        value = scaled_tile(left(), w_ref, e_ref, start, depth, at, width)
        place = pl.ds(offset + at, width)
        if first:
            acc_ref[:, place] = value
        else:
            acc_ref[:, place] = acc_ref[:, place] + value

    full = columns // TILE

    def step(index, carry):
        one(pl.multiple_of(index * TILE, TILE), TILE)
        return carry

    lax.fori_loop(0, full, step, 0)
    if columns % TILE:
        one(full * TILE, columns % TILE)


def gelu(x):
    return 0.5 * x * (1.0 + lax.erf(x * (1.0 / math.sqrt(2.0))))


def layer_kernel(
    n_dm, n_df,
    lengths_ref, hidden_ref, norm_ref, turn_ref,
    wq_hbm, eq_hbm, wkv_hbm, ekv_hbm, wo_hbm, eo_hbm, wu_hbm, eu_hbm, wd_hbm, ed_hbm, cache_hbm,
    out_ref,
    wq, eq, wkv, ekv, wo, eo, wbig, eu, ed, cache,
    attn_x, mlp_x, resid, stat, qacc, qsend, qrecv, hsend, hrecv, qs, kvn, sc, ob,
    osend, orecv, aall, att, upacc, upsend, uprecv, act, tot, fsend, frecv,
    local_sem, s_stat, r_stat, s_q, r_q, s_h, r_h, s_o, r_o, s_a, r_a, s_u, r_u, s_g, r_g, s_f, r_f,
):
    rows, width = hidden_ref.shape
    q_cols = wq.shape[1]
    units = wu_hbm.shape[1]
    slots = cache.shape[1]
    part_rows = rows // n_dm
    me_m = lax.axis_index("dm")
    me_f = lax.axis_index("df")

    def along_m(step):
        return lax.rem(me_m + step, n_dm)

    def along_f(step):
        return lax.rem(me_f + step, n_df)

    def to_m(source, target, send, recv, step):
        return pltpu.make_async_remote_copy(
            src_ref=source, dst_ref=target, send_sem=send.at[step], recv_sem=recv.at[step],
            device_id=(along_m(step), me_f), device_id_type=pl.DeviceIdType.MESH,
        )

    def to_f(source, target, send, recv, step):
        return pltpu.make_async_remote_copy(
            src_ref=source, dst_ref=target, send_sem=send.at[step], recv_sem=recv.at[step],
            device_id=(me_m, along_f(step)), device_id_type=pl.DeviceIdType.MESH,
        )

    def local(source, target, index):
        return pltpu.make_async_copy(source, target, local_sem.at[index])

    load_q = [local(wq_hbm, wq, 0), local(eq_hbm, eq, 1), local(wkv_hbm, wkv, 2),
              local(ekv_hbm, ekv, 3)]
    load_eu = local(eu_hbm, eu, 4)
    load_ed = local(ed_hbm, ed, 5)
    load_o = [local(wo_hbm, wo, 6), local(eo_hbm, eo, 7)]
    load_c = local(cache_hbm, cache, 8)
    up_parts = pieces(width, DEEP)
    down_parts = pieces(units, DEEP)
    load_up = [local(wu_hbm.at[pl.ds(a, s)], wbig.at[pl.ds(a, s)], 9 + i)
               for i, (a, s) in enumerate(up_parts)]
    base = 9 + len(up_parts)
    load_down = [local(wd_hbm.at[pl.ds(a, s)], wbig.at[pl.ds(a, s)], base + i)
                 for i, (a, s) in enumerate(down_parts)]

    for copy in load_q:
        copy.start()
    load_eu.start()
    load_up[0].start()

    barrier = pltpu.get_barrier_semaphore()
    for step in range(1, n_dm):
        pl.semaphore_signal(barrier, inc=1, device_id=(along_m(step), me_f),
                            device_id_type=pl.DeviceIdType.MESH)
    for step in range(1, n_df):
        pl.semaphore_signal(barrier, inc=1, device_id=(me_m, along_f(step)),
                            device_id_type=pl.DeviceIdType.MESH)

    wide = hidden_ref[...].astype(F32)
    sums = jnp.sum(wide, axis=1, keepdims=True)
    squares = jnp.sum(wide * wide, axis=1, keepdims=True)
    lane16 = lax.broadcasted_iota(jnp.int32, (rows, LANES), 1)
    stat[0] = jnp.where(lane16 == 0, sums, jnp.where(lane16 == 1, squares, 0.0))

    pl.semaphore_wait(barrier, n_dm - 1 + n_df - 1)

    stat_copies = [to_m(stat.at[0], stat.at[step], s_stat, r_stat, step) for step in range(1, n_dm)]
    for copy in stat_copies:
        copy.start()
    tot[:, :width] = wide
    tot[:, width:] = jnp.zeros((rows, tot.shape[1] - width), F32)
    share = width // n_df
    span = resid.shape[2]

    def window(index):
        at = index * share
        low = at // LANES * LANES
        value = tot[:, low:low + span + LANES]
        if at > low:
            value = pltpu.roll(value, span + LANES - (at - low), 1)
        return value[:, :span]

    for index in range(n_df):
        resid[index] = window(index)
    qsend[...] = jnp.zeros_like(qsend)
    osend[...] = jnp.zeros_like(osend)
    upacc[:, units:] = jnp.zeros((rows, upacc.shape[1] - units), F32)
    for copy in stat_copies:
        copy.wait()
    both = stat[0]
    for step in range(1, n_dm):
        both = both + stat[step]
    features = float(width * n_dm)
    mean = both[:, 0:1] / features
    inverse = lax.rsqrt(both[:, 1:2] / features - mean * mean + epsilon)
    normed = (hidden_ref[...].astype(F32) - mean) * inverse
    attn_x[...] = (normed * norm_ref[0:1, :] + norm_ref[1:2, :]).astype(BF16)
    mlp_x[...] = (normed * norm_ref[2:3, :] + norm_ref[3:4, :]).astype(BF16)

    load_up[1].start()
    for copy in load_q:
        copy.wait()
    for index, (start, depth) in enumerate(up_parts):
        def left(start=start, depth=depth):
            return attn_x[:, start:start + depth]
        scaled_into(qacc, 0, index == 0, left, wq, eq, start, depth, q_cols)
        scaled_into(qacc, q_cols, index == 0, left, wkv, ekv, start, depth, wkv.shape[1])
    for index in range(n_dm):
        qsend[index, 0:part_rows, :] = qacc[index * part_rows:(index + 1) * part_rows, :]
    q_copies = [to_m(qsend.at[along_m(step)], qrecv.at[step], s_q, r_q, step)
                for step in range(1, n_dm)]
    for copy in q_copies:
        copy.start()

    def up(index):
        start, depth = up_parts[index]
        load_up[index].wait()
        scaled_into(upacc, 0, index == 0, lambda: mlp_x[:, start:start + depth],
                    wbig, eu, start, depth, units)

    load_up[2].start()
    load_up[3].start()
    load_eu.wait()
    up(0)
    load_c.start()

    for copy in q_copies:
        copy.wait()
    mine = qsend[me_m]
    for step in range(1, n_dm):
        mine = mine + qrecv[step]
    lane = lax.broadcasted_iota(jnp.int32, (8, LANES), 1)
    low_half = lane < HD
    cosine = turn_ref[0]
    sine = turn_ref[1]

    def rope(value):
        partner = jnp.where(lane % HD < HD // 2, pltpu.roll(value, LANES - HD // 2, 1),
                            pltpu.roll(value, HD // 2, 1))
        return value * cosine + partner * sine

    def rounded(value):
        return value.astype(BF16).astype(F32)

    new = mine[:, q_cols:q_cols + LANES]
    kvn[...] = rounded(jnp.where(low_half, rope(new), new))
    roped = [rope(mine[:, at:at + LANES]) for at in range(0, q_cols, LANES)]
    half = len(roped) // 2
    for group in range(n_df):
        early, late = roped[group // 2], roped[half + group // 2]
        if group % 2 == 0:
            hsend[group] = jnp.where(low_half, early, pltpu.roll(late, HD, 1))
        else:
            hsend[group] = jnp.where(low_half, pltpu.roll(early, HD, 1), late)
    h_copies = [to_f(hsend.at[along_f(step)], hrecv.at[step], s_h, r_h, step)
                for step in range(1, n_df)]
    for copy in h_copies:
        copy.start()

    load_down[0].start()
    load_ed.start()
    up(1)
    load_down[1].start()
    up(2)
    load_down[2].start()
    for copy in load_o:
        copy.start()
    up(3)
    load_down[3].start()
    for index in range(n_dm):
        upsend[index] = upacc[:, index * DEEP:(index + 1) * DEEP].astype(BF16)
    u_copies = [to_m(upsend.at[along_m(step)], uprecv.at[step], s_u, r_u, step)
                for step in range(1, n_dm)]
    for copy in u_copies:
        copy.start()

    for copy in h_copies:
        copy.wait()
    for step in range(n_df):
        value = hsend[me_f] if step == 0 else hrecv[step]
        first = jnp.where(low_half, value, 0.0)
        second = jnp.where(low_half, pltpu.roll(value, HD, 1), 0.0)
        for row in range(part_rows):
            at = row * 2 * n_df + 2 * step
            qs[at:at + 1, :] = first[row:row + 1, :]
            qs[at + 1:at + 2, :] = second[row:row + 1, :]
    load_c.wait()
    heads = 2 * n_df
    factor = 1.0 / math.sqrt(HD)

    def attend(row, carry):
        place = pl.ds(pl.multiple_of(row * heads, heads), heads)
        query = qs[place, :].astype(BF16)
        own_kv = kvn[pl.ds(row, 1), :]
        own = jnp.sum(query.astype(F32) * own_kv, axis=1, keepdims=True) * factor
        top = own
        limit = lengths_ref[row]
        for start, depth in pieces(slots, DEEP):
            score = lax.dot_general(
                query, cache[row, pl.ds(start, depth), :], (((1,), (1,)), ((), ())),
                preferred_element_type=F32,
            ) * factor
            live = start + lax.broadcasted_iota(jnp.int32, (heads, depth), 1) < limit
            score = jnp.where(live, score, -1e30)
            sc[:, pl.ds(start, depth)] = score
            top = jnp.maximum(top, jnp.max(score, axis=1, keepdims=True))
        own_weight = jnp.exp(own - top)
        total = own_weight
        summed = rounded(own_weight) * own_kv
        for start, depth in pieces(slots, DEEP):
            live = start + lax.broadcasted_iota(jnp.int32, (heads, depth), 1) < limit
            weight = jnp.where(live, jnp.exp(sc[:, pl.ds(start, depth)] - top), 0.0)
            total = total + jnp.sum(weight, axis=1, keepdims=True)
            summed = summed + jnp.dot(
                weight.astype(BF16), cache[row, pl.ds(start, depth), :],
                preferred_element_type=F32,
            )
        ob[place, :] = summed / total
        return carry

    lax.fori_loop(0, part_rows, attend, 0)
    for step in range(n_df):
        for row in range(part_rows):
            at = row * heads + 2 * step
            pair = jnp.where(low_half[0:1], pltpu.roll(ob[at:at + 1, :], HD, 1), ob[at + 1:at + 2, :])
            osend[step, row:row + 1, :] = pair
    o_copies = [
        pltpu.make_async_remote_copy(
            src_ref=osend.at[step], dst_ref=orecv.at[me_f], send_sem=s_o.at[step],
            recv_sem=r_o.at[step], device_id=(me_m, along_f(n_df - step)),
            device_id_type=pl.DeviceIdType.MESH,
        )
        for step in range(1, n_df)
    ]
    for copy in o_copies:
        copy.start()

    for copy in u_copies:
        copy.wait()
    units_mine = upsend[me_m].astype(F32)
    for step in range(1, n_dm):
        units_mine = units_mine + uprecv[step].astype(F32)
    act[me_m] = gelu(units_mine).astype(BF16)
    g_copies = [to_m(act.at[me_m], act.at[me_m], s_g, r_g, step) for step in range(1, n_dm)]
    for copy in g_copies:
        copy.start()

    orecv[me_f] = osend[0]
    for copy in o_copies:
        copy.wait()
    pack = []
    for index in range(n_df // 2):
        even, odd = orecv[2 * index], orecv[2 * index + 1]
        aall[me_m, :, index * LANES:(index + 1) * LANES] = jnp.where(
            low_half, even, pltpu.roll(odd, HD, 1))
        at = (half + index) * LANES
        aall[me_m, :, at:at + LANES] = jnp.where(low_half, pltpu.roll(even, HD, 1), odd)
    a_copies = [to_m(aall.at[me_m], aall.at[me_m], s_a, r_a, step) for step in range(1, n_dm)]
    for copy in a_copies:
        copy.start()

    for copy in g_copies:
        copy.wait()
    load_ed.wait()

    def down(index):
        start, depth = down_parts[index]
        load_down[index].wait()
        scaled_into(tot, 0, index == 0, lambda: act[index, :, :depth], wbig, ed, start, depth, width)

    down(0)
    for copy in a_copies:
        copy.wait()
    for index in range(n_dm):
        att[index * part_rows:(index + 1) * part_rows, :] = aall[index, 0:part_rows, :]
    for copy in load_o:
        copy.wait()
    down(1)
    scaled_into(tot, 0, False, lambda: att[...].astype(BF16), wo, eo, 0, q_cols, width)
    down(2)
    down(3)

    for index in range(n_df):
        fsend[index] = window(index).astype(BF16)
    f_copies = [to_f(fsend.at[along_f(step)], frecv.at[step], s_f, r_f, step)
                for step in range(1, n_df)]
    for copy in f_copies:
        copy.start()
    result = resid[me_f] + fsend[me_f].astype(F32)
    for step, copy in enumerate(f_copies):
        copy.wait()
        result = result + frecv[step + 1].astype(F32)
    out_ref[...] = result[:, :share].astype(BF16)


def fits(mesh, arrays):
    rows, width = arrays[0].shape
    n_dm, n_df = mesh.shape["dm"], mesh.shape["df"]
    local, queries, units = width // n_dm, arrays[5].shape[1] // n_df, arrays[11].shape[1] // n_df
    return (
        n_df == KV and HEADS == 16 * KV and queries == DEEP and local == units
        and rows // n_dm <= 8 and rows % 16 == 0 and local % LANES == 0
        and len(pieces(local, DEEP)) == 4 and n_dm == 4
    )


def fused(
    n_dm, n_df, hidden_in, attn_gain, attn_bias, mlp_gain, mlp_bias, w_query, query_exp,
    w_keyval, keyval_exp, w_out, out_exp, w_up, up_exp, w_down, down_exp, kv_cache, lengths,
    positions,
):
    rows, width = hidden_in.shape
    part_rows = rows // n_dm
    norm = jnp.stack([attn_gain, attn_bias, mlp_gain, mlp_bias])
    half = HD // 2
    freqs = jnp.power(10000.0, -2.0 * jnp.arange(half, dtype=F32) / HD)
    angles = positions.astype(F32)[:, None] * freqs[None, :]
    cosine, sine = jnp.cos(angles), jnp.sin(angles)
    turn = jnp.stack([
        jnp.concatenate([cosine] * 4, axis=1), jnp.concatenate([-sine, sine] * 2, axis=1),
    ])
    turn = jnp.pad(turn, ((0, 0), (0, 8 - part_rows), (0, 0)))
    q_cols, kv_cols, units = w_query.shape[1], w_keyval.shape[1], w_up.shape[1]
    heads = HEADS // KV
    slots = kv_cache.shape[1]
    share = width // n_df
    span = -(-share // LANES) * LANES
    wide_total = (n_df - 1) * share // LANES * LANES + span + LANES
    vmem = pltpu.VMEM
    sem = pltpu.SemaphoreType.DMA
    scratch = [
        vmem(w_query.shape, BF16), vmem(query_exp.shape, jnp.int32),
        vmem(w_keyval.shape, BF16), vmem(keyval_exp.shape, jnp.int32),
        vmem(w_out.shape, BF16), vmem(out_exp.shape, jnp.int32),
        vmem((max(width, units), max(width, units)), BF16),
        vmem(up_exp.shape, jnp.int32), vmem(down_exp.shape, jnp.int32),
        vmem(kv_cache.shape, BF16),
        vmem((rows, width), BF16), vmem((rows, width), BF16), vmem((n_df, rows, span), F32),
        vmem((n_dm, rows, LANES), F32),
        vmem((rows, q_cols + kv_cols), F32), vmem((n_dm, 8, q_cols + kv_cols), F32),
        vmem((n_dm, 8, q_cols + kv_cols), F32),
        vmem((n_df, 8, LANES), F32), vmem((n_df, 8, LANES), F32),
        vmem((part_rows * heads, LANES), F32), vmem((8, LANES), F32),
        vmem((heads, slots), F32), vmem((part_rows * heads, LANES), F32),
        vmem((n_df, 8, LANES), F32), vmem((n_df, 8, LANES), F32),
        vmem((n_dm, 8, q_cols), F32), vmem((rows, q_cols), F32),
        vmem((rows, n_dm * DEEP), F32), vmem((n_dm, rows, DEEP), BF16),
        vmem((n_dm, rows, DEEP), BF16), vmem((n_dm, rows, DEEP), BF16),
        vmem((rows, wide_total), F32), vmem((n_df, rows, span), BF16),
        vmem((n_df, rows, span), BF16),
        sem((17,)),
        sem((n_dm,)), sem((n_dm,)), sem((n_dm,)), sem((n_dm,)), sem((n_df,)), sem((n_df,)),
        sem((n_df,)), sem((n_df,)), sem((n_dm,)), sem((n_dm,)), sem((n_dm,)), sem((n_dm,)),
        sem((n_dm,)), sem((n_dm,)), sem((n_df,)), sem((n_df,)),
    ]
    in_vmem = pl.BlockSpec(memory_space=pltpu.VMEM)
    in_any = pl.BlockSpec(memory_space=pl.ANY)
    return pl.pallas_call(
        functools.partial(layer_kernel, n_dm, n_df),
        out_shape=jax.ShapeDtypeStruct((rows, share), BF16),
        in_specs=[pl.BlockSpec(memory_space=pltpu.SMEM)] + [in_vmem] * 3 + [in_any] * 11,
        out_specs=in_vmem,
        scratch_shapes=scratch,
        compiler_params=pltpu.CompilerParams(
            collective_id=0, has_side_effects=True, vmem_limit_bytes=62 * 2**20
        ),
    )(
        lengths, hidden_in, norm, turn, w_query, query_exp, w_keyval, keyval_exp, w_out, out_exp,
        w_up, up_exp, w_down, down_exp, kv_cache,
    )


def solution(mesh):
    def whole(*arrays):
        body = on_device
        if fits(mesh, arrays):
            body = functools.partial(fused, mesh.shape["dm"], mesh.shape["df"])
        return mapped(mesh, body)(*arrays)

    return whole


def mapped(mesh, body):
    return jax.shard_map(
        body,
        mesh=mesh,
        in_specs=(
            P(None, "dm"),
            P("dm"),
            P("dm"),
            P("dm"),
            P("dm"),
            P("dm", "df"),
            P("dm", "df"),
            P("dm", "df"),
            P("dm", "df"),
            P("df", "dm"),
            P("df", "dm"),
            P("dm", "df"),
            P("dm", "df"),
            P("df", "dm"),
            P("df", "dm"),
            P("dm", "df", None),
            P("dm"),
            P("dm"),
        ),
        out_specs=P(None, ("dm", "df")),
        check_vma=False,
    )
```

```python
import functools
import math

import jax
import jax.numpy as jnp
from jax import lax
from jax.experimental import pallas as pl
from jax.experimental.pallas import tpu as pltpu
from jax.sharding import PartitionSpec as P

D = 14848
HEADS = 128
KV = 8
HD = 64


epsilon = 1e-05


def merged(part, axis, combine):
    gathered = jax.tree.map(lambda a: lax.all_gather(a, axis), part)

    def take(source):
        return jax.tree.map(lambda a: lax.dynamic_index_in_dim(a, source, 0, False), gathered)

    return lax.fori_loop(
        1, lax.axis_size(axis), lambda source, state: combine(state, take(source)), take(0)
    )


def powers(exponents):
    return jnp.where(
        exponents == -2, 0.25, jnp.where(exponents == -1, 0.5, jnp.where(exponents == 0, 1.0, 2.0))
    ).astype(jnp.bfloat16)


def dequantize(weight, exponents):
    depth, width_out = weight.shape
    slabs = weight.reshape(depth // 32, 32, width_out) * powers(exponents)[:, None, :]
    return slabs.reshape(depth, width_out)


def rotate(values, places):
    half = HD // 2
    freqs = jnp.power(10000.0, -2.0 * jnp.arange(half, dtype=jnp.float32) / HD)
    angles = places.astype(jnp.float32)[:, None] * freqs[None, :]
    cosine = jnp.cos(angles)[:, None, :]
    sine = jnp.sin(angles)[:, None, :]
    first_half = values[..., :half]
    second_half = values[..., half:]
    return jnp.concatenate(
        [first_half * cosine - second_half * sine, second_half * cosine + first_half * sine],
        axis=-1,
    )


def join_parts(earlier, later):
    top_early, den_early, acc_early = earlier
    top_late, den_late, acc_late = later
    highest = jnp.maximum(top_early, top_late)
    fade_early = jnp.exp(top_early - highest)
    fade_late = jnp.exp(top_late - highest)
    return (
        highest,
        den_early * fade_early + den_late * fade_late,
        acc_early * fade_early[..., None] + acc_late * fade_late[..., None],
    )


def on_device(
    hidden_in,
    attn_gain,
    attn_bias,
    mlp_gain,
    mlp_bias,
    w_query,
    query_exp,
    w_keyval,
    keyval_exp,
    w_out,
    out_exp,
    w_up,
    up_exp,
    w_down,
    down_exp,
    kv_cache,
    lengths,
    positions,
):
    row_count, local_width = hidden_in.shape
    wide = hidden_in.astype(jnp.float32)
    total_sum, square_sum = lax.psum((jnp.sum(wide, axis=1), jnp.sum(wide * wide, axis=1)), "dm")
    mean_value = (total_sum / D)[:, None]
    inverse = lax.rsqrt(square_sum[:, None] / D - mean_value * mean_value + epsilon)
    normed = (wide - mean_value) * inverse
    attn_in = (normed * attn_gain + attn_bias).astype(jnp.bfloat16)
    mlp_in = (normed * mlp_gain + mlp_bias).astype(jnp.bfloat16)
    query_w = dequantize(w_query, query_exp)
    keyval_w = dequantize(w_keyval, keyval_exp)
    query_cols = query_w.shape[1]
    part_rows = row_count // lax.axis_size("dm")
    projected = lax.psum_scatter(
        jnp.concatenate(
            [
                jnp.dot(attn_in, query_w, preferred_element_type=jnp.float32),
                jnp.dot(attn_in, keyval_w, preferred_element_type=jnp.float32),
            ],
            axis=1,
        ),
        "dm",
        scatter_dimension=0,
        tiled=True,
    )
    query_all, keyval_all = (
        lax.all_gather(projected[:, :query_cols], "df", axis=1, tiled=True),
        lax.all_gather(projected[:, query_cols:], "df", axis=1, tiled=True),
    )
    queries = rotate(query_all.reshape(part_rows, HEADS, HD), positions).astype(jnp.bfloat16)
    keyval_new = keyval_all.reshape(part_rows, KV, 2, HD)
    new_keys = rotate(keyval_new[:, :, 0], positions).astype(jnp.bfloat16)
    new_values = keyval_new[:, :, 1].astype(jnp.bfloat16)
    head_devices = lax.axis_size("df")
    blocks = head_devices // KV
    column = lax.axis_index("df")
    group = column // blocks
    block = column % blocks
    group_size = HEADS // KV
    heads_each = HEADS // head_devices
    slots = kv_cache.shape[1]
    factor = 1.0 / math.sqrt(HD)
    query_group = lax.dynamic_slice_in_dim(
        queries.reshape(part_rows, group_size, KV, HD), group, 1, 2
    )[:, :, 0]
    key_one = lax.dynamic_slice_in_dim(new_keys, group, 1, 1)[:, 0]
    value_one = lax.dynamic_slice_in_dim(new_values, group, 1, 1)[:, 0]
    cache_keys = kv_cache[:, :, :HD]
    cache_values = kv_cache[:, :, HD:]
    scores = (
        jnp.einsum("rgd,rcd->rgc", query_group, cache_keys, preferred_element_type=jnp.float32)
        * factor
    )
    places = block * slots + jnp.arange(slots, dtype=jnp.int32)
    live = (places[None, :] < lengths[:, None])[:, None, :]
    scores = jnp.where(live, scores, -1e30)
    leading = block == 0
    own_scores = (
        jnp.einsum("rgd,rd->rg", query_group, key_one, preferred_element_type=jnp.float32) * factor
    )
    own_scores = jnp.where(leading, own_scores, -1e30)
    top_score = jnp.maximum(jnp.max(scores, axis=-1), own_scores)
    weights = jnp.where(live, jnp.exp(scores - top_score[..., None]), 0.0)
    own_weights = jnp.where(leading, jnp.exp(own_scores - top_score), 0.0)
    denominator = jnp.sum(weights, axis=-1) + own_weights
    summed = jnp.einsum(
        "rgc,rcd->rgd",
        weights.astype(jnp.bfloat16),
        cache_values,
        preferred_element_type=jnp.float32,
    )
    summed = (
        summed
        + own_weights.astype(jnp.bfloat16).astype(jnp.float32)[..., None]
        * value_one.astype(jnp.float32)[:, None, :]
    )
    selector = jnp.arange(KV, dtype=jnp.int32) == group
    acc_full = jnp.where(selector[None, None, :, None], summed[:, :, None, :], 0.0).reshape(
        part_rows, HEADS, HD
    )
    top_full = jnp.where(selector[None, None, :], top_score[:, :, None], -1e30).reshape(
        part_rows, HEADS
    )
    den_full = jnp.where(selector[None, None, :], denominator[:, :, None], 0.0).reshape(
        part_rows, HEADS
    )
    top_all, den_all, acc_all = merged((top_full, den_full, acc_full), "df", join_parts)
    own_acc = lax.dynamic_slice_in_dim(acc_all, column * heads_each, heads_each, 1)
    own_den = lax.dynamic_slice_in_dim(den_all, column * heads_each, heads_each, 1)
    attended = (
        (own_acc / own_den[..., None]).reshape(part_rows, heads_each * HD).astype(jnp.bfloat16)
    )
    out_w = dequantize(w_out, out_exp)
    attention_part = jnp.dot(
        lax.all_gather(attended, "dm", axis=0, tiled=True),
        out_w,
        preferred_element_type=jnp.float32,
    )
    up_w = dequantize(w_up, up_exp)
    down_w = dequantize(w_down, down_exp)
    up_total = lax.psum(jnp.dot(mlp_in, up_w, preferred_element_type=jnp.float32), "dm")
    activated = jax.nn.gelu(up_total, approximate=False).astype(jnp.bfloat16)
    feed_part = jnp.dot(activated, down_w, preferred_element_type=jnp.float32)
    layer_total = lax.psum_scatter(
        attention_part + feed_part, "df", scatter_dimension=1, tiled=True
    )
    slice_width = local_width // head_devices
    residual = lax.dynamic_slice_in_dim(wide, column * slice_width, slice_width, 1)
    return (residual + layer_total).astype(jnp.bfloat16)


BLOCK = 32
DEEP = 1024
TILE = 1024
DEPTH = 256
UNROLL = True
LANES = 128
F32 = jnp.float32
BF16 = jnp.bfloat16


def pieces(length, step):
    return [(at, min(step, length - at)) for at in range(0, length, step)]


def powers_wide(exponents):
    return jnp.where(
        exponents == -2, 0.25, jnp.where(exponents == -1, 0.5, jnp.where(exponents == 0, 1.0, 2.0))
    )


def scaled_tile(left, w_ref, e_ref, start, depth, at, width):
    total = None
    for low, span in pieces(depth, DEPTH):
        exps = e_ref[pl.ds((start + low) // BLOCK, span // BLOCK), pl.ds(at, width)]
        scale = jnp.broadcast_to(
            powers_wide(exps)[:, None, :], (span // BLOCK, BLOCK, width)
        ).astype(BF16).reshape(span, width)
        weight = w_ref[pl.ds(start + low, span), pl.ds(at, width)] * scale
        part = jnp.dot(left[:, low:low + span], weight, preferred_element_type=F32)
        total = part if total is None else total + part
    return total


def scaled_into(acc_ref, offset, first, left, w_ref, e_ref, start, depth, columns):
    def one(at, width):
        value = scaled_tile(left(), w_ref, e_ref, start, depth, at, width)
        place = pl.ds(offset + at, width)
        if first:
            acc_ref[:, place] = value
        else:
            acc_ref[:, place] = acc_ref[:, place] + value

    full = columns // TILE

    def step(index, carry):
        one(pl.multiple_of(index * TILE, TILE), TILE)
        return carry

    lax.fori_loop(0, full, step, 0, unroll=UNROLL)
    if columns % TILE:
        one(full * TILE, columns % TILE)


def gelu(x):
    return 0.5 * x * (1.0 + lax.erf(x * (1.0 / math.sqrt(2.0))))


def layer_kernel(
    n_dm, n_df,
    lengths_ref, positions_ref, hidden_ref, again_ref, abias_ref, mgain_ref, mbias_ref,
    wq_hbm, eq_hbm, wkv_hbm, ekv_hbm, wo_hbm, eo_hbm, wu_hbm, eu_hbm, wd_hbm, ed_hbm, cache_hbm,
    out_ref,
    wq, eq, wkv, ekv, wo, eo, wbig, eu, ed, cache,
    attn_x, mlp_x, resid, stat, qacc, qsend, qrecv, hsend, hrecv, qs, kvn, sc, ob,
    osend, orecv, aall, att, upacc, upsend, uprecv, act, tot, fsend, frecv,
    local_sem, s_stat, r_stat, s_q, r_q, s_h, r_h, s_o, r_o, s_a, r_a, s_u, r_u, s_g, r_g, s_f, r_f,
):
    rows, width = hidden_ref.shape
    q_cols = wq.shape[1]
    units = wu_hbm.shape[1]
    slots = cache.shape[1]
    part_rows = rows // n_dm
    me_m = lax.axis_index("dm")
    me_f = lax.axis_index("df")

    def along_m(step):
        return lax.rem(me_m + step, n_dm)

    def along_f(step):
        return lax.rem(me_f + step, n_df)

    def to_m(source, target, send, recv, step):
        return pltpu.make_async_remote_copy(
            src_ref=source, dst_ref=target, send_sem=send.at[step], recv_sem=recv.at[step],
            device_id=(along_m(step), me_f), device_id_type=pl.DeviceIdType.MESH,
        )

    def to_f(source, target, send, recv, step):
        return pltpu.make_async_remote_copy(
            src_ref=source, dst_ref=target, send_sem=send.at[step], recv_sem=recv.at[step],
            device_id=(me_m, along_f(step)), device_id_type=pl.DeviceIdType.MESH,
        )

    def local(source, target, index):
        return pltpu.make_async_copy(source, target, local_sem.at[index])

    load_q = [local(wq_hbm, wq, 0), local(eq_hbm, eq, 1), local(wkv_hbm, wkv, 2),
              local(ekv_hbm, ekv, 3)]
    load_eu = local(eu_hbm, eu, 4)
    load_ed = local(ed_hbm, ed, 5)
    load_o = [local(wo_hbm, wo, 6), local(eo_hbm, eo, 7)]
    load_c = local(cache_hbm, cache, 8)
    up_parts = pieces(width, DEEP)
    down_parts = pieces(units, DEEP)
    load_up = [local(wu_hbm.at[pl.ds(a, s)], wbig.at[pl.ds(a, s)], 9 + i)
               for i, (a, s) in enumerate(up_parts)]
    base = 9 + len(up_parts)
    load_down = [local(wd_hbm.at[pl.ds(a, s)], wbig.at[pl.ds(a, s)], base + i)
                 for i, (a, s) in enumerate(down_parts)]

    for copy in load_q:
        copy.start()
    load_eu.start()
    load_up[0].start()
    load_up[1].start()

    barrier = pltpu.get_barrier_semaphore()
    for step in range(1, n_dm):
        pl.semaphore_signal(barrier, inc=1, device_id=(along_m(step), me_f),
                            device_id_type=pl.DeviceIdType.MESH)
    for step in range(1, n_df):
        pl.semaphore_signal(barrier, inc=1, device_id=(me_m, along_f(step)),
                            device_id_type=pl.DeviceIdType.MESH)

    wide = hidden_ref[...].astype(F32)
    sums = jnp.sum(wide, axis=1, keepdims=True)
    squares = jnp.sum(wide * wide, axis=1, keepdims=True)
    lane16 = lax.broadcasted_iota(jnp.int32, (rows, LANES), 1)
    stat[0] = jnp.where(lane16 == 0, sums, jnp.where(lane16 == 1, squares, 0.0))

    pl.semaphore_wait(barrier, n_dm - 1 + n_df - 1)

    stat_copies = [to_m(stat.at[0], stat.at[step], s_stat, r_stat, step) for step in range(1, n_dm)]
    for copy in stat_copies:
        copy.start()
    tot[:, :width] = wide
    tot[:, width:] = jnp.zeros((rows, tot.shape[1] - width), F32)
    share = width // n_df
    span = resid.shape[2]

    def flat(ref):
        return ref[...].reshape(1, width)

    def window(index):
        at = index * share
        low = at // LANES * LANES
        value = tot[:, low:low + span + LANES]
        if at > low:
            value = pltpu.roll(value, span + LANES - (at - low), 1)
        return value[:, :span]

    for index in range(n_df):
        resid[index] = window(index)
    qsend[...] = jnp.zeros_like(qsend)
    osend[...] = jnp.zeros_like(osend)
    upacc[:, units:] = jnp.zeros((rows, upacc.shape[1] - units), F32)
    for copy in stat_copies:
        copy.wait()
    both = stat[0]
    for step in range(1, n_dm):
        both = both + stat[step]
    features = float(width * n_dm)
    mean = both[:, 0:1] / features
    inverse = lax.rsqrt(both[:, 1:2] / features - mean * mean + epsilon)
    normed = (hidden_ref[...].astype(F32) - mean) * inverse
    attn_x[...] = (normed * flat(again_ref) + flat(abias_ref)).astype(BF16)
    mlp_x[...] = (normed * flat(mgain_ref) + flat(mbias_ref)).astype(BF16)

    for copy in load_q:
        copy.wait()
    scaled_into(qacc, 0, True, lambda: attn_x[...], wq, eq, 0, width, q_cols)
    scaled_into(qacc, q_cols, True, lambda: attn_x[...], wkv, ekv, 0, width, wkv.shape[1])
    for index in range(n_dm):
        qsend[index, 0:part_rows, :] = qacc[index * part_rows:(index + 1) * part_rows, :]
    q_copies = [to_m(qsend.at[along_m(step)], qrecv.at[step], s_q, r_q, step)
                for step in range(1, n_dm)]
    for copy in q_copies:
        copy.start()

    def up(index):
        start, depth = up_parts[index]
        load_up[index].wait()
        scaled_into(upacc, 0, index == 0, lambda: mlp_x[:, start:start + depth],
                    wbig, eu, start, depth, units)

    load_up[2].start()
    load_up[3].start()
    load_eu.wait()
    up(0)
    load_c.start()
    load_ed.start()
    load_down[0].start()
    up(1)
    load_down[1].start()

    for copy in q_copies:
        copy.wait()
    mine = qsend[me_m]
    for step in range(1, n_dm):
        mine = mine + qrecv[step]
    lane = lax.broadcasted_iota(jnp.int32, (8, LANES), 1)
    low_half = lane < HD
    row8 = lax.broadcasted_iota(jnp.int32, (8, LANES), 0)
    place8 = jnp.zeros((8, LANES), jnp.int32)
    for row in range(part_rows):
        place8 = jnp.where(row8 == row, positions_ref[row], place8)
    freqs = jnp.zeros((8, LANES), F32)
    for index in range(HD // 2):
        freqs = jnp.where(lane % (HD // 2) == index, 10000.0 ** (-2.0 * index / HD), freqs)
    angles = place8.astype(F32) * freqs
    cosine = jnp.cos(angles)
    sine = jnp.where(lane % HD < HD // 2, -1.0, 1.0) * jnp.sin(angles)

    def rope(value):
        partner = jnp.where(lane % HD < HD // 2, pltpu.roll(value, LANES - HD // 2, 1),
                            pltpu.roll(value, HD // 2, 1))
        return value * cosine + partner * sine

    def rounded(value):
        return value.astype(BF16).astype(F32)

    new = mine[:, q_cols:q_cols + LANES]
    kvn[...] = rounded(jnp.where(low_half, rope(new), new))
    roped = [rope(mine[:, at:at + LANES]) for at in range(0, q_cols, LANES)]
    half = len(roped) // 2
    for group in range(n_df):
        early, late = roped[group // 2], roped[half + group // 2]
        if group % 2 == 0:
            hsend[group] = jnp.where(low_half, early, pltpu.roll(late, HD, 1))
        else:
            hsend[group] = jnp.where(low_half, pltpu.roll(early, HD, 1), late)
    h_copies = [to_f(hsend.at[along_f(step)], hrecv.at[step], s_h, r_h, step)
                for step in range(1, n_df)]
    for copy in h_copies:
        copy.start()

    up(2)
    load_down[2].start()
    for copy in load_o:
        copy.start()
    up(3)
    load_down[3].start()
    for index in range(n_dm):
        upsend[index] = upacc[:, index * DEEP:(index + 1) * DEEP].astype(BF16)
    u_copies = [to_m(upsend.at[along_m(step)], uprecv.at[step], s_u, r_u, step)
                for step in range(1, n_dm)]
    for copy in u_copies:
        copy.start()

    for copy in h_copies:
        copy.wait()
    for step in range(n_df):
        value = hsend[me_f] if step == 0 else hrecv[step]
        first = jnp.where(low_half, value, 0.0)
        second = jnp.where(low_half, pltpu.roll(value, HD, 1), 0.0)
        for row in range(part_rows):
            at = row * 2 * n_df + 2 * step
            qs[at:at + 1, :] = first[row:row + 1, :]
            qs[at + 1:at + 2, :] = second[row:row + 1, :]
    load_c.wait()
    heads = 2 * n_df
    factor = 1.0 / math.sqrt(HD)

    def attend(row, carry):
        place = pl.ds(pl.multiple_of(row * heads, heads), heads)
        query = qs[place, :].astype(BF16)
        own_kv = kvn[pl.ds(row, 1), :]
        own = jnp.sum(query.astype(F32) * own_kv, axis=1, keepdims=True) * factor
        top = own
        limit = lengths_ref[row]
        for start, depth in pieces(slots, DEEP):
            score = lax.dot_general(
                query, cache[row, pl.ds(start, depth), :], (((1,), (1,)), ((), ())),
                preferred_element_type=F32,
            ) * factor
            live = start + lax.broadcasted_iota(jnp.int32, (heads, depth), 1) < limit
            score = jnp.where(live, score, -1e30)
            sc[:, pl.ds(start, depth)] = score
            top = jnp.maximum(top, jnp.max(score, axis=1, keepdims=True))
        own_weight = jnp.exp(own - top)
        total = own_weight
        summed = rounded(own_weight) * own_kv
        for start, depth in pieces(slots, DEEP):
            live = start + lax.broadcasted_iota(jnp.int32, (heads, depth), 1) < limit
            weight = jnp.where(live, jnp.exp(sc[:, pl.ds(start, depth)] - top), 0.0)
            total = total + jnp.sum(weight, axis=1, keepdims=True)
            summed = summed + jnp.dot(
                weight.astype(BF16), cache[row, pl.ds(start, depth), :],
                preferred_element_type=F32,
            )
        ob[place, :] = summed / total
        return carry

    lax.fori_loop(0, part_rows // 2, attend, 0, unroll=True)

    for copy in u_copies:
        copy.wait()
    units_mine = upsend[me_m].astype(F32)
    for step in range(1, n_dm):
        units_mine = units_mine + uprecv[step].astype(F32)
    act[me_m] = gelu(units_mine).astype(BF16)
    g_copies = [to_m(act.at[me_m], act.at[me_m], s_g, r_g, step) for step in range(1, n_dm)]
    for copy in g_copies:
        copy.start()

    lax.fori_loop(part_rows // 2, part_rows, attend, 0, unroll=True)
    for step in range(n_df):
        for row in range(part_rows):
            at = row * heads + 2 * step
            pair = jnp.where(low_half[0:1], pltpu.roll(ob[at:at + 1, :], HD, 1), ob[at + 1:at + 2, :])
            osend[step, row:row + 1, :] = pair
    o_copies = [
        pltpu.make_async_remote_copy(
            src_ref=osend.at[step], dst_ref=orecv.at[me_f], send_sem=s_o.at[step],
            recv_sem=r_o.at[step], device_id=(me_m, along_f(n_df - step)),
            device_id_type=pl.DeviceIdType.MESH,
        )
        for step in range(1, n_df)
    ]
    for copy in o_copies:
        copy.start()

    for copy in g_copies:
        copy.wait()
    load_ed.wait()

    def down(index):
        start, depth = down_parts[index]
        load_down[index].wait()
        scaled_into(tot, 0, index == 0, lambda: act[index, :, :depth], wbig, ed, start, depth, width)

    down(0)
    down(1)
    orecv[me_f] = osend[0]
    for copy in o_copies:
        copy.wait()
    for index in range(n_df // 2):
        even, odd = orecv[2 * index], orecv[2 * index + 1]
        aall[me_m, :, index * LANES:(index + 1) * LANES] = jnp.where(
            low_half, even, pltpu.roll(odd, HD, 1))
        at = (half + index) * LANES
        aall[me_m, :, at:at + LANES] = jnp.where(low_half, pltpu.roll(even, HD, 1), odd)
    a_copies = [to_m(aall.at[me_m], aall.at[me_m], s_a, r_a, step) for step in range(1, n_dm)]
    for copy in a_copies:
        copy.start()
    down(2)
    for copy in a_copies:
        copy.wait()
    for index in range(n_dm):
        att[index * part_rows:(index + 1) * part_rows, :] = aall[index, 0:part_rows, :]
    for copy in load_o:
        copy.wait()
    scaled_into(tot, 0, False, lambda: att[...].astype(BF16), wo, eo, 0, q_cols, width)
    down(3)

    for index in range(n_df):
        fsend[index] = window(index).astype(BF16)
    f_copies = [to_f(fsend.at[along_f(step)], frecv.at[step], s_f, r_f, step)
                for step in range(1, n_df)]
    for copy in f_copies:
        copy.start()
    result = resid[me_f] + fsend[me_f].astype(F32)
    for step, copy in enumerate(f_copies):
        copy.wait()
        result = result + frecv[step + 1].astype(F32)
    out_ref[...] = result[:, :share].astype(BF16)


def fits(mesh, arrays):
    rows, width = arrays[0].shape
    n_dm, n_df = mesh.shape["dm"], mesh.shape["df"]
    local, queries, units = width // n_dm, arrays[5].shape[1] // n_df, arrays[11].shape[1] // n_df
    return (
        n_df == KV and HEADS == 16 * KV and queries == DEEP and local == units
        and rows // n_dm <= 8 and rows % 16 == 0 and local % LANES == 0
        and len(pieces(local, DEEP)) == 4 and n_dm == 4
    )


def fused(
    n_dm, n_df, hidden_in, attn_gain, attn_bias, mlp_gain, mlp_bias, w_query, query_exp,
    w_keyval, keyval_exp, w_out, out_exp, w_up, up_exp, w_down, down_exp, kv_cache, lengths,
    positions,
):
    rows, width = hidden_in.shape
    part_rows = rows // n_dm
    q_cols, kv_cols, units = w_query.shape[1], w_keyval.shape[1], w_up.shape[1]
    heads = HEADS // KV
    slots = kv_cache.shape[1]
    share = width // n_df
    span = -(-share // LANES) * LANES
    wide_total = (n_df - 1) * share // LANES * LANES + span + LANES
    vmem = pltpu.VMEM
    sem = pltpu.SemaphoreType.DMA
    scratch = [
        vmem(w_query.shape, BF16), vmem(query_exp.shape, jnp.int32),
        vmem(w_keyval.shape, BF16), vmem(keyval_exp.shape, jnp.int32),
        vmem(w_out.shape, BF16), vmem(out_exp.shape, jnp.int32),
        vmem((max(width, units), max(width, units)), BF16),
        vmem(up_exp.shape, jnp.int32), vmem(down_exp.shape, jnp.int32),
        vmem(kv_cache.shape, BF16),
        vmem((rows, width), BF16), vmem((rows, width), BF16), vmem((n_df, rows, span), F32),
        vmem((n_dm, rows, LANES), F32),
        vmem((rows, q_cols + kv_cols), F32), vmem((n_dm, 8, q_cols + kv_cols), F32),
        vmem((n_dm, 8, q_cols + kv_cols), F32),
        vmem((n_df, 8, LANES), F32), vmem((n_df, 8, LANES), F32),
        vmem((part_rows * heads, LANES), F32), vmem((8, LANES), F32),
        vmem((heads, slots), F32), vmem((part_rows * heads, LANES), F32),
        vmem((n_df, 8, LANES), F32), vmem((n_df, 8, LANES), F32),
        vmem((n_dm, 8, q_cols), F32), vmem((rows, q_cols), F32),
        vmem((rows, n_dm * DEEP), F32), vmem((n_dm, rows, DEEP), BF16),
        vmem((n_dm, rows, DEEP), BF16), vmem((n_dm, rows, DEEP), BF16),
        vmem((rows, wide_total), F32), vmem((n_df, rows, span), BF16),
        vmem((n_df, rows, span), BF16),
        sem((17,)),
        sem((n_dm,)), sem((n_dm,)), sem((n_dm,)), sem((n_dm,)), sem((n_df,)), sem((n_df,)),
        sem((n_df,)), sem((n_df,)), sem((n_dm,)), sem((n_dm,)), sem((n_dm,)), sem((n_dm,)),
        sem((n_dm,)), sem((n_dm,)), sem((n_df,)), sem((n_df,)),
    ]
    in_vmem = pl.BlockSpec(memory_space=pltpu.VMEM)
    in_any = pl.BlockSpec(memory_space=pl.ANY)
    return pl.pallas_call(
        functools.partial(layer_kernel, n_dm, n_df),
        out_shape=jax.ShapeDtypeStruct((rows, share), BF16),
        in_specs=[pl.BlockSpec(memory_space=pltpu.SMEM)] * 2 + [in_vmem] * 5 + [in_any] * 11,
        out_specs=in_vmem,
        scratch_shapes=scratch,
        compiler_params=pltpu.CompilerParams(
            collective_id=0, has_side_effects=True, vmem_limit_bytes=62 * 2**20
        ),
    )(
        lengths, positions, hidden_in, attn_gain, attn_bias, mlp_gain, mlp_bias, w_query, query_exp, w_keyval, keyval_exp, w_out, out_exp,
        w_up, up_exp, w_down, down_exp, kv_cache,
    )


def solution(mesh):
    def whole(*arrays):
        body = on_device
        if fits(mesh, arrays):
            body = functools.partial(fused, mesh.shape["dm"], mesh.shape["df"])
        return mapped(mesh, body)(*arrays)

    return whole


def mapped(mesh, body):
    return jax.shard_map(
        body,
        mesh=mesh,
        in_specs=(
            P(None, "dm"),
            P("dm"),
            P("dm"),
            P("dm"),
            P("dm"),
            P("dm", "df"),
            P("dm", "df"),
            P("dm", "df"),
            P("dm", "df"),
            P("df", "dm"),
            P("df", "dm"),
            P("dm", "df"),
            P("dm", "df"),
            P("df", "dm"),
            P("df", "dm"),
            P("dm", "df", None),
            P("dm"),
            P("dm"),
        ),
        out_specs=P(None, ("dm", "df")),
        check_vma=False,
    )
```
